512 devices in a mesh: dp: 4 (over z_hi, core), expert: 16 (over z_lo, x), tensor: 8 (over y).
Axes of the slice: x: 4, y: 8, z: 8 (z_hi: 2, z_lo: 4; z = z_hi * 4 + z_lo), core: 2. Of those that a mesh axis runs over, the one named last changes fastest.
Arguments:
- x_rows: bfloat16 [1536, 3072], P(('dp', 'expert'), 'tensor'), may hold values from -6 to 6
- cotangent: bfloat16 [1536, 3072], P(('dp', 'expert'), 'tensor'), may hold values from -6 to 6
- expert_ids: int32 [1536, 4], P(('dp', 'expert')), may hold values from 0 to 15, all different within a row; in each aligned block of 24 rows (0 to 23, 24 to 47, ...) at most 8 rows name the same one
- route_weight: float32 [1536, 4], P(('dp', 'expert')), may hold values from 0.1 to 1
- gate_weight: bfloat16 [16, 3072, 5376], P('expert', 'dp', 'tensor'), may hold values from -0.109375 to 0.109375
- up_weight: bfloat16 [16, 3072, 5376], P('expert', 'dp', 'tensor'), may hold values from -0.109375 to 0.109375
- down_weight: bfloat16 [16, 5376, 3072], P('expert', 'tensor', 'dp'), may hold values from -0.078125 to 0.078125
Outputs:
- input_grad: bfloat16 [1536, 3072], P(('dp', 'expert'), 'tensor')
- down_grad: bfloat16 [16, 5376, 3072], P('expert', 'tensor', 'dp')
The draws below stay inside these ranges and needn't reach their ends.
Inputs may be any that keep to these rules, and one draw needn't show every extreme that they name: `expert_ids`: each token names 4 different experts. In each aligned block of 24 rows (the tokens of one index of dp and expert) no expert is named by more than 8 rows, a bound that some block reaches.
All inputs are finite; a program needn't handle non-finite values.
Results may differ from the reference program's by a relative error of at most 0.0064.
Values may be sent and summed in bfloat16 or wider, within the bound.
No kernel may reach another device: no remote copies, remote signals or barrier semaphores. Data moves between devices by JAX's collectives and lax.ppermute only.
A program may use at most 64 MiB of HBM per device.

```python
import math
import jax
import jax.numpy as jnp
import numpy as np
from jax import lax

D = 3072
FF = 5376
E = 16
TOPK = 4
TOK_GRP = 24
CAP = 8
TOKENS = 1536


def block_scale(rng, shape, pieces, least, high):
    factor_of = 1.0
    for axis_at, blocks in pieces:
        draws = jax.random.uniform(jax.random.fold_in(jax.random.fold_in(rng, 6), axis_at), (blocks,), jnp.float32, least / len(pieces), high / len(pieces))
        factor_of = factor_of * jnp.repeat(jnp.exp(draws), shape[axis_at] // blocks).reshape((-1,) + (1,) * (len(shape) - 1 - axis_at))
    return factor_of


def shared_out(stream_key, own, number, rows, amount, top, limit, slope):
    order = jax.random.permutation(stream_key, amount)
    heavy_load, usual = shares(amount, rows * top, limit, slope, True), shares(amount, rows * top, limit, slope, False)
    places = jnp.arange(amount)

    def named(sizes, turn):
        used = int((sizes > 0).sum())
        fixed = max(1, used // 4)
        shifted = fixed + (places - fixed + turn * (used - fixed)) % max(1, amount - fixed)
        return jnp.zeros((amount,), jnp.int32).at[order[jnp.where(places < fixed, places, shifted)]].set(jnp.asarray(sizes, jnp.int32))

    sizes = jnp.where(number % 4 == 0, named(heavy_load, number // 4), named(usual, number - number // 4 - 1))
    mixed = jax.random.permutation(jax.random.fold_in(own, 3), amount)
    donor, receiver = mixed[0:amount // 2 * 2:2], mixed[1:amount // 2 * 2:2]
    room = jnp.minimum(sizes[donor] - 1, limit - sizes[receiver]) // 2
    room = jnp.where((donor == order[0]) | (receiver == order[0]) | (sizes[receiver] == 0), 0, jnp.maximum(room, 0))
    shifted = jax.random.randint(jax.random.fold_in(own, 4), (amount // 2,), 0, 1 << 20) % (room + 1)
    sizes = sizes.at[donor].add(-shifted).at[receiver].add(shifted)
    labels = jnp.searchsorted(jnp.cumsum(sizes), jnp.arange(rows * top), side="right").astype(jnp.int32)
    grid = labels.reshape(top, rows).T
    grid = grid[jax.random.permutation(jax.random.fold_in(own, 1), rows)]
    turn = jax.random.randint(jax.random.fold_in(own, 2), (rows, 1), 0, top)
    return jnp.take_along_axis(grid, (jnp.arange(top)[None, :] + turn) % top, axis=1)


def shares(amount, total, most, lean, full):
    weights = [(1 << 20) // math.isqrt(rank ** lean) + 1 for rank in range(1, amount + 1)]
    largest = most if full else min(most, max(-(-total // amount), total * weights[0] // sum(weights)))
    least = 1 if total - largest >= amount - 1 else 0
    holding, surplus = [largest] + [least] * (amount - 1), total - largest - least * (amount - 1)
    while surplus > 0:
        free = [i for i in range(1, amount) if holding[i] < largest] or [i for i in range(1, amount) if holding[i] < most]
        pool, left = sum([weights[i] for i in free]), surplus
        for i in free:
            more = min(most - holding[i], max(1, left * weights[i] // pool), surplus)
            holding[i] = holding[i] + more
            surplus = surplus - more
    return np.array(holding)


def bell_draw(stream_key, extent, spread, bound, cuts=(), kind=jnp.bfloat16):
    drawn = jax.random.normal(stream_key, extent, jnp.float32) * spread
    if len(cuts) > 0:
        drawn = block_scale(stream_key, extent, cuts, -0.22, 0.18) * drawn
    return jnp.clip(drawn, min=-bound, max=bound).astype(kind)


def setup_inputs(seed: int = 0) -> dict:
    keys = jax.random.split(jax.random.key(seed), 8)
    x_rows = bell_draw(keys[0], (TOKENS, D), 1.0, 6.0, ((0, 64), (1, 8)))
    cotangent = bell_draw(keys[1], (TOKENS, D), 1.0, 6.0, ((0, 64), (1, 8)))
    expert_ids_keys = jax.random.split(jax.random.fold_in(keys[2], 1), TOKENS // TOK_GRP)
    expert_ids_turns = jax.random.permutation(jax.random.fold_in(keys[2], 3), TOKENS // TOK_GRP)
    expert_ids = jax.vmap(lambda own, number: shared_out(jax.random.fold_in(keys[2], 2), own, number, TOK_GRP, E, TOPK, CAP, 1))(expert_ids_keys, expert_ids_turns).reshape((TOKENS, TOPK))
    route_weight = jnp.clip(0.1 + 0.9 * jax.random.uniform(keys[3], (TOKENS, TOPK), jnp.float32) ** block_scale(keys[3], (TOKENS, TOPK), ((0, 64),), -0.2, 0.2), 0.1, 1.0)
    gate_weight = bell_draw(keys[4], (E, D, FF), D ** -0.5, 0.109375, ((0, 16), (1, 4), (2, 8)))
    up_weight = bell_draw(keys[5], (E, D, FF), D ** -0.5, 0.109375, ((0, 16), (1, 4), (2, 8)))
    down_weight = bell_draw(keys[6], (E, FF, D), FF ** -0.5, 0.078125, ((0, 16), (1, 8), (2, 4)))
    return {"x_rows": x_rows, "cotangent": cotangent, "expert_ids": expert_ids, "route_weight": route_weight, "gate_weight": gate_weight, "up_weight": up_weight, "down_weight": down_weight}


def expert_step(items):
    rows_x, rows_dy, w_gate, w_up, w_down = items
    gate = jnp.dot(rows_x, w_gate, preferred_element_type=jnp.float32)
    up = jnp.dot(rows_x, w_up, preferred_element_type=jnp.float32)
    sigma = jax.nn.sigmoid(gate)
    active = gate * sigma
    hidden = (active * up).astype(jnp.bfloat16)
    hidden_grad = jnp.dot(rows_dy, w_down.T, preferred_element_type=jnp.float32)
    down_grad = jnp.dot(hidden.T, rows_dy, preferred_element_type=jnp.float32).astype(jnp.bfloat16)
    gate_grad = (hidden_grad * up * sigma * (1.0 + gate * (1.0 - sigma))).astype(jnp.bfloat16)
    up_grad = (hidden_grad * active).astype(jnp.bfloat16)
    row_grad = jnp.dot(gate_grad, w_gate.T, preferred_element_type=jnp.float32)
    row_grad = (row_grad + jnp.dot(up_grad, w_up.T, preferred_element_type=jnp.float32)).astype(jnp.bfloat16)
    return row_grad, down_grad


def reference(x_rows, cotangent, expert_ids, route_weight, gate_weight, up_weight, down_weight):
    blocks = TOKENS // TOK_GRP
    ids = expert_ids.reshape(blocks, TOK_GRP, TOPK)
    weights = route_weight.reshape(blocks, TOK_GRP, TOPK)
    onehot = (ids[..., None] == jnp.arange(E, dtype=jnp.int32)).astype(jnp.int32)
    per_token = jnp.sum(onehot, axis=2)
    before = jnp.cumsum(per_token, axis=1) - per_token
    slot = jnp.sum(onehot * before[:, :, None, :], axis=3).astype(jnp.int32)
    target = (ids * CAP + slot).astype(jnp.int32)
    block_index = jnp.broadcast_to(jnp.arange(blocks, dtype=jnp.int32)[:, None, None], target.shape)
    x_blocks = x_rows.reshape(blocks, TOK_GRP, D)
    dy_blocks = cotangent.reshape(blocks, TOK_GRP, D)
    x_copies = jnp.broadcast_to(x_blocks[:, :, None, :], (blocks, TOK_GRP, TOPK, D))
    scaled = (weights[..., None] * dy_blocks[:, :, None, :].astype(jnp.float32)).astype(jnp.bfloat16)
    dispatched_x = jnp.zeros((blocks, E * CAP, D), jnp.bfloat16).at[block_index, target].set(x_copies)
    dispatched_dy = jnp.zeros((blocks, E * CAP, D), jnp.bfloat16).at[block_index, target].set(scaled)
    rows_x = dispatched_x.reshape(blocks, E, CAP, D).transpose(1, 0, 2, 3).reshape(E, blocks * CAP, D)
    rows_dy = dispatched_dy.reshape(blocks, E, CAP, D).transpose(1, 0, 2, 3).reshape(E, blocks * CAP, D)
    row_grad, down_grad = lax.map(expert_step, (rows_x, rows_dy, gate_weight, up_weight, down_weight))
    slots_back = row_grad.reshape(E, blocks, CAP, D).transpose(1, 0, 2, 3).reshape(blocks, E * CAP, D)
    picked = slots_back[block_index, target].astype(jnp.float32)
    input_grad = jnp.sum(picked, axis=2).astype(jnp.bfloat16).reshape(TOKENS, D)
    return input_grad, down_grad
```

```python
import jax
import jax.numpy as jnp
from jax import lax
from jax.sharding import Mesh, PartitionSpec as P

CAP = 8
BF16 = jnp.bfloat16
F32 = jnp.float32
AXES = ("z_hi", "core", "z_lo", "x", "tensor")
BLOCKS = ("z_hi", "core", "z_lo", "x")
EXPERT = ("z_lo", "x")
SIDES = ("z_hi", "z_lo", "x")
SWAP = [(0, 1), (1, 0)]


def route_tables(expert_ids, route_weight, experts, capacity):
    onehot = (expert_ids[:, :, None] == jnp.arange(experts, dtype=jnp.int32)[None, None, :]).astype(
        jnp.int32
    )
    per_token = jnp.sum(onehot, axis=1)
    before = jnp.cumsum(per_token, axis=0) - per_token
    slot = jnp.sum(onehot * before[:, None, :], axis=2)
    target = expert_ids * capacity + slot
    places = jnp.arange(experts * capacity, dtype=jnp.int32)
    match = (target[:, :, None] == places[None, None, :]).astype(F32)
    select = jnp.sum(match, axis=1).astype(BF16)
    slot_weight = jnp.sum(match * route_weight[:, :, None], axis=(0, 1))
    return (select, slot_weight)


def dot(a, b, ca, cb):
    return lax.dot_general(a, b, (((ca,), (cb,)), ((), ())), preferred_element_type=F32)


def order_quarters(value, axis):
    shape = value.shape
    halves = value.reshape(shape[:axis] + (2, 2, shape[axis] // 4) + shape[axis + 1 :])
    flipped = jnp.flip(halves, axis=axis + 1)
    return jnp.where(lax.axis_index("core") == 0, halves, flipped).reshape(shape)


def per_device(x_rows, cotangent, expert_ids, route_weight, gate_weight, up_weight, down_weight):
    tensor = lax.axis_size("tensor")
    experts = lax.axis_size(EXPERT)
    tokens, piece = x_rows.shape
    own_gate, own_up, own_down = gate_weight[0], up_weight[0], down_weight[0]
    far_gate, far_up, far_down = (
        lax.ppermute(own_gate, "core", SWAP),
        lax.ppermute(own_up, "core", SWAP),
        lax.ppermute(own_down, "core", SWAP),
    )
    quarter = own_gate.shape[0]
    hidden_units = own_gate.shape[1]

    both = jnp.concatenate([x_rows, cotangent], axis=0)
    both = lax.all_to_all(
        jnp.broadcast_to(both[None], (tensor,) + both.shape), "tensor", 0, 0, tiled=True
    )
    both = order_quarters(both, 0)
    both = jnp.transpose(both, (1, 0, 2)).reshape(2 * tokens, tensor * piece)
    select, slot_weight = route_tables(expert_ids, route_weight, experts, CAP)
    places = experts * CAP

    def dispatch(rows, scale):
        halves = [
            dot(select, rows[:, z * 2 * quarter : (z + 1) * 2 * quarter], 0, 0) for z in range(2)
        ]
        if scale is not None:
            halves = [half * scale[:, None] for half in halves]
        sent = jnp.concatenate([half.astype(BF16) for half in halves], axis=0)
        got = lax.all_to_all(
            sent.reshape(2 * experts, CAP, 2 * quarter), SIDES, 0, 0, tiled=True
        )
        return got.reshape(2 * places, 2 * quarter)

    got_x = dispatch(both[:tokens], None)
    gate = dot(own_gate, got_x[:, :quarter], 0, 1) + dot(far_gate, got_x[:, quarter:], 0, 1)
    up = dot(own_up, got_x[:, :quarter], 0, 1) + dot(far_up, got_x[:, quarter:], 0, 1)
    crossed = lax.ppermute(
        jnp.concatenate([gate.astype(BF16), up.astype(BF16)], axis=0), "z_hi", SWAP
    )
    got_dy = dispatch(both[tokens:], slot_weight)
    swapped_dy = lax.ppermute(got_dy[:, quarter:], "core", SWAP)
    hidden_grad = dot(own_down, got_dy[:, :quarter], 1, 1) + dot(
        far_down, got_dy[:, quarter:], 1, 1
    )
    crossed_grad = lax.ppermute(hidden_grad.astype(BF16), "z_hi", SWAP)

    gate = gate + crossed[:hidden_units].astype(F32)
    up = up + crossed[hidden_units:].astype(F32)
    sigma = jax.nn.sigmoid(gate)
    active = gate * sigma
    hidden = (active * up).astype(BF16)
    swapped_hidden = lax.ppermute(hidden, "core", SWAP)
    slope = up * sigma * (1.0 + gate * (1.0 - sigma))
    hidden_grad = hidden_grad + crossed_grad.astype(F32)
    gate_grad = (hidden_grad * slope).astype(BF16)
    up_grad = (hidden_grad * active).astype(BF16)

    own_term = dot(gate_grad, own_gate, 0, 1) + dot(up_grad, own_up, 0, 1)
    far_term = dot(gate_grad, far_gate, 0, 1) + dot(up_grad, far_up, 0, 1)
    term = jnp.concatenate([own_term.astype(BF16), far_term.astype(BF16)], axis=1)
    returned = lax.all_to_all(
        term.reshape(2 * experts, CAP, 2 * quarter), SIDES, 0, 0, tiled=True
    ).reshape(2, places, 2 * quarter)
    mixed = jnp.concatenate([dot(select, returned[z], 1, 0) for z in range(2)], axis=1)
    mixed = jnp.transpose(mixed.astype(BF16).reshape(tokens, tensor, piece), (1, 0, 2))
    mixed = lax.all_to_all(order_quarters(mixed, 0), "tensor", 0, 0, tiled=True)
    input_grad = jnp.sum(mixed.astype(F32), axis=0).astype(BF16)

    down_grad = dot(hidden, got_dy[:, :quarter], 1, 0) + dot(swapped_hidden, swapped_dy, 1, 0)
    return (input_grad, down_grad.astype(BF16)[None])


def solution(mesh):
    fine = Mesh(mesh.devices.reshape(2, 2, 4, 4, 8), AXES)
    placed = (
        P(BLOCKS, "tensor"),
        P(BLOCKS, "tensor"),
        P(BLOCKS, None),
        P(BLOCKS, None),
        P(EXPERT, ("z_hi", "core"), "tensor"),
        P(EXPERT, ("z_hi", "core"), "tensor"),
        P(EXPERT, "tensor", ("z_hi", "core")),
    )
    return jax.shard_map(
        per_device,
        mesh=fine,
        in_specs=placed,
        out_specs=(P(BLOCKS, "tensor"), P(EXPERT, "tensor", ("z_hi", "core"))),
        check_vma=False,
    )
```

```python
import jax
import jax.numpy as jnp
from jax import lax
from jax.experimental import pallas as pl
from jax.experimental.pallas import tpu as pltpu
from jax.sharding import Mesh, PartitionSpec as P

CAP = 8
BF16 = jnp.bfloat16
F32 = jnp.float32
AXES = ("z_hi", "core", "z_lo", "x", "tensor")
BLOCKS = ("z_hi", "core", "z_lo", "x")
EXPERT = ("z_lo", "x")
SIDES = ("z_hi", "z_lo", "x")
SWAP = [(0, 1), (1, 0)]


def route_tables(expert_ids, route_weight, experts, capacity):
    onehot = (expert_ids[:, :, None] == jnp.arange(experts, dtype=jnp.int32)[None, None, :]).astype(
        jnp.int32
    )
    per_token = jnp.sum(onehot, axis=1)
    before = jnp.cumsum(per_token, axis=0) - per_token
    slot = jnp.sum(onehot * before[:, None, :], axis=2)
    target = expert_ids * capacity + slot
    places = jnp.arange(experts * capacity, dtype=jnp.int32)
    match = (target[:, :, None] == places[None, None, :]).astype(F32)
    select = jnp.sum(match, axis=1).astype(BF16)
    slot_weight = jnp.sum(match * route_weight[:, :, None], axis=(0, 1))
    return (select, slot_weight)


def dot(a, b, ca, cb):
    return lax.dot_general(a, b, (((ca,), (cb,)), ((), ())), preferred_element_type=F32)


def order_quarters(value, axis):
    shape = value.shape
    halves = value.reshape(shape[:axis] + (2, 2, shape[axis] // 4) + shape[axis + 1 :])
    flipped = jnp.flip(halves, axis=axis + 1)
    return jnp.where(lax.axis_index("core") == 0, halves, flipped).reshape(shape)


def params():
    return pltpu.CompilerParams(vmem_limit_bytes=40 * 1024 * 1024)


def cost(flops, moved):
    return pl.CostEstimate(flops=flops, bytes_accessed=moved, transcendentals=0)


def gate_up_body(own_gate, far_gate, own_up, far_up, own_x, far_x, exact, rounded):
    for i, (own, far) in enumerate(((own_gate, far_gate), (own_up, far_up))):
        value = dot(own[...], own_x[...], 1, 1) + dot(far[...], far_x[...], 1, 1)
        exact[i] = value
        rounded[i] = value.astype(BF16)


def gate_up_product(own_gate, far_gate, own_up, far_up, rows):
    hidden, quarter = own_gate.shape
    count = rows.shape[0]
    step = hidden // 3
    weight = pl.BlockSpec((step, quarter), lambda i: (i, 0))
    out = pl.BlockSpec((2, step, count), lambda i: (0, i, 0))
    return pl.pallas_call(
        gate_up_body,
        grid=(3,),
        in_specs=[weight] * 4
        + [
            pl.BlockSpec((count, quarter), lambda i: (0, 0)),
            pl.BlockSpec((count, quarter), lambda i: (0, 1)),
        ],
        out_specs=[out, out],
        out_shape=[
            jax.ShapeDtypeStruct((2, hidden, count), F32),
            jax.ShapeDtypeStruct((2, hidden, count), BF16),
        ],
        compiler_params=params(),
        cost_estimate=cost(8 * hidden * quarter * count, 8 * hidden * quarter),
    )(own_gate, far_gate, own_up, far_up, rows, rows)


def hidden_grad_body(own_down, far_down, own_dy, far_dy, exact, rounded):
    value = dot(own_down[...], own_dy[...], 1, 0) + dot(far_down[...], far_dy[...], 1, 0)
    exact[...] = value
    rounded[...] = value.astype(BF16)


def hidden_grad_product(own_down, far_down, columns):
    hidden, quarter = own_down.shape
    count = columns.shape[1]
    step = hidden // 3
    weight = pl.BlockSpec((step, quarter), lambda i: (i, 0))
    out = pl.BlockSpec((step, count), lambda i: (i, 0))
    return pl.pallas_call(
        hidden_grad_body,
        grid=(3,),
        in_specs=[weight] * 2
        + [
            pl.BlockSpec((quarter, count), lambda i: (0, 0)),
            pl.BlockSpec((quarter, count), lambda i: (1, 0)),
        ],
        out_specs=[out, out],
        out_shape=[
            jax.ShapeDtypeStruct((hidden, count), F32),
            jax.ShapeDtypeStruct((hidden, count), BF16),
        ],
        compiler_params=params(),
        cost_estimate=cost(4 * hidden * quarter * count, 4 * hidden * quarter),
    )(own_down, far_down, columns, columns)


def row_grad_body(
    exact, crossed, slope, active, own_gate, far_gate, own_up, far_up, out, own_sum, far_sum
):
    @pl.when(pl.program_id(0) == 0)
    def _():
        own_sum[...] = jnp.zeros_like(own_sum)
        far_sum[...] = jnp.zeros_like(far_sum)

    grad = exact[...] + crossed[...].astype(F32)
    gate_grad = (grad * slope[...]).astype(BF16)
    up_grad = (grad * active[...]).astype(BF16)
    own_sum[...] += dot(gate_grad, own_gate[...], 0, 0) + dot(up_grad, own_up[...], 0, 0)
    far_sum[...] += dot(gate_grad, far_gate[...], 0, 0) + dot(up_grad, far_up[...], 0, 0)

    @pl.when(pl.program_id(0) == pl.num_programs(0) - 1)
    def _():
        quarter = own_sum.shape[1]
        out[:, :quarter] = own_sum[...].astype(BF16)
        out[:, quarter:] = far_sum[...].astype(BF16)


def row_grad_product(exact, crossed, slope, active, own_gate, far_gate, own_up, far_up):
    hidden, quarter = own_gate.shape
    count = exact.shape[1]
    step = hidden // 3
    weight = pl.BlockSpec((step, quarter), lambda i: (i, 0))
    value = pl.BlockSpec((step, count), lambda i: (i, 0))
    return pl.pallas_call(
        row_grad_body,
        grid=(3,),
        in_specs=[value] * 4 + [weight] * 4,
        out_specs=pl.BlockSpec((count, 2 * quarter), lambda i: (0, 0)),
        out_shape=jax.ShapeDtypeStruct((count, 2 * quarter), BF16),
        scratch_shapes=[pltpu.VMEM((count, quarter), F32)] * 2,
        compiler_params=params(),
        cost_estimate=cost(8 * hidden * quarter * count, 8 * hidden * quarter),
    )(exact, crossed, slope, active, own_gate, far_gate, own_up, far_up)


def per_device(x_rows, cotangent, expert_ids, route_weight, gate_weight, up_weight, down_weight):
    tensor = lax.axis_size("tensor")
    experts = lax.axis_size(EXPERT)
    tokens, piece = x_rows.shape
    places = experts * CAP
    half = gate_weight.shape[1] * 2
    chunk = half // tensor
    own_gate, own_up, own_down = gate_weight[0].T, up_weight[0].T, down_weight[0]

    both = jnp.concatenate([x_rows, cotangent], axis=0)
    both = lax.all_to_all(
        jnp.broadcast_to(both[None], (tensor,) + both.shape), "tensor", 0, 0, tiled=True
    )
    select, slot_weight = route_tables(expert_ids, route_weight, experts, CAP)
    far_gate, far_up, far_down = (
        lax.ppermute(own_gate, "core", SWAP),
        lax.ppermute(own_up, "core", SWAP),
        lax.ppermute(own_down, "core", SWAP),
    )

    both = jnp.transpose(order_quarters(both, 0), (1, 0, 2)).reshape(2 * tokens, 2 * half)
    turn = lax.axis_index("tensor")
    sent = []
    for z in range(2):
        part = both[:, z * half : (z + 1) * half]
        dy = lax.dynamic_slice_in_dim(part[tokens:], turn * chunk, chunk, axis=1)
        dy = dot(select, dy, 0, 0) * slot_weight[:, None]
        dy = jnp.pad(dy, ((0, 0), (0, 256 - chunk)))
        sent.append(
            jnp.concatenate([dot(select, part[:tokens], 0, 0).astype(BF16), dy.astype(BF16)], axis=1)
        )
    sent = jnp.stack(sent).reshape(2 * experts, CAP, half + 256)
    got = lax.all_to_all(sent, SIDES, 0, 0, tiled=True).reshape(2 * places, half + 256)

    gate_up, gate_up_sent = gate_up_product(own_gate, far_gate, own_up, far_up, got)
    crossed = lax.ppermute(gate_up_sent, "z_hi", SWAP)
    got_dy = lax.all_gather(got[:, half : half + chunk].T, "tensor", axis=0, tiled=True)
    hidden_grad, hidden_grad_sent = hidden_grad_product(own_down, far_down, got_dy)
    crossed_grad = lax.ppermute(hidden_grad_sent, "z_hi", SWAP)
    swapped_dy = lax.ppermute(got_dy[half // 2 :], "core", SWAP)

    gate_up = gate_up + crossed.astype(F32)
    gate, up = gate_up[0], gate_up[1]
    sigma = jax.nn.sigmoid(gate)
    active = gate * sigma
    hidden = (active * up).astype(BF16)
    swapped_hidden = lax.ppermute(hidden, "core", SWAP)
    slope = up * sigma * (1.0 + gate * (1.0 - sigma))

    term = row_grad_product(
        hidden_grad, crossed_grad, slope, active, own_gate, far_gate, own_up, far_up
    )
    returned = lax.all_to_all(
        term.reshape(2 * experts, CAP, half), SIDES, 0, 0, tiled=True
    ).reshape(2, places, half)
    mixed = jnp.concatenate([dot(select, returned[z], 1, 0) for z in range(2)], axis=1)
    mixed = jnp.transpose(mixed.astype(BF16).reshape(tokens, tensor, piece), (1, 0, 2))
    mixed = lax.all_to_all(order_quarters(mixed, 0), "tensor", 0, 0, tiled=True)
    input_grad = jnp.sum(mixed.astype(F32), axis=0).astype(BF16)

    down_grad = dot(hidden, got_dy[: half // 2], 1, 1) + dot(swapped_hidden, swapped_dy, 1, 1)
    return (input_grad, down_grad.astype(BF16)[None])


def solution(mesh):
    fine = Mesh(mesh.devices.reshape(2, 2, 4, 4, 8), AXES)
    placed = (
        P(BLOCKS, "tensor"),
        P(BLOCKS, "tensor"),
        P(BLOCKS, None),
        P(BLOCKS, None),
        P(EXPERT, ("z_hi", "core"), "tensor"),
        P(EXPERT, ("z_hi", "core"), "tensor"),
        P(EXPERT, "tensor", ("z_hi", "core")),
    )
    return jax.shard_map(
        per_device,
        mesh=fine,
        in_specs=placed,
        out_specs=(P(BLOCKS, "tensor"), P(EXPERT, "tensor", ("z_hi", "core"))),
        check_vma=False,
    )
```

```python
import functools

import jax
import jax.numpy as jnp
from jax import lax
from jax.experimental import pallas as pl
from jax.experimental.pallas import tpu as pltpu
from jax.sharding import Mesh, PartitionSpec as P

CAP = 8
BF16 = jnp.bfloat16
F32 = jnp.float32
AXES = ("z_hi", "core", "z_lo", "x", "tensor")
BLOCKS = ("z_hi", "core", "z_lo", "x")
EXPERT = ("z_lo", "x")
SIDES = ("z_hi", "z_lo", "x")
SWAP = [(0, 1), (1, 0)]


def route_tables(expert_ids, route_weight, experts, capacity):
    onehot = (expert_ids[:, :, None] == jnp.arange(experts, dtype=jnp.int32)[None, None, :]).astype(
        jnp.int32
    )
    per_token = jnp.sum(onehot, axis=1)
    before = jnp.cumsum(per_token, axis=0) - per_token
    slot = jnp.sum(onehot * before[:, None, :], axis=2)
    target = expert_ids * capacity + slot
    places = jnp.arange(experts * capacity, dtype=jnp.int32)
    select = jnp.sum((target[:, :, None] == places[None, None, :]).astype(F32), axis=1).astype(BF16)
    match = (target.T[None] == places[:, None, None]).astype(F32)
    gather = jnp.sum(match, axis=1).astype(BF16)
    slot_weight = jnp.sum(match * route_weight.T[None], axis=(1, 2))
    return (select, gather, slot_weight[:, None])


def dot(a, b, ca, cb):
    return lax.dot_general(a, b, (((ca,), (cb,)), ((), ())), preferred_element_type=F32)


def params():
    return pltpu.CompilerParams(vmem_limit_bytes=16 * 1024 * 1024)


def in_hbm(*arrays):
    return [pltpu.with_memory_space_constraint(array, pltpu.HBM) for array in arrays]


def in_vmem(*arrays):
    return [pltpu.with_memory_space_constraint(array, pltpu.VMEM) for array in arrays]


def cost(flops, moved):
    return pl.CostEstimate(flops=flops, bytes_accessed=moved, transcendentals=0)


def spread_body(x_rows, cotangent, out):
    tokens, piece = x_rows.shape
    half = piece // 2
    blank = jnp.zeros((tokens, out.shape[2] - piece - half), BF16)
    for j in range(2):
        part = jnp.concatenate([cotangent[:, j * half : (j + 1) * half], blank], axis=1)
        for i in range(j, out.shape[0], 2):
            out[i, :, :piece] = x_rows[...]
            out[i, :, piece:] = part


def spread(x_rows, cotangent, tensor):
    tokens, piece = x_rows.shape
    vmem = pl.BlockSpec(memory_space=pltpu.VMEM)
    return pl.pallas_call(
        spread_body,
        in_specs=[vmem] * 2,
        out_specs=vmem,
        out_shape=pltpu.HBM((tensor, tokens, piece + 256), BF16),
        compiler_params=params(),
        cost_estimate=cost(0, 600000),
    )(*in_hbm(x_rows, cotangent))


def dispatch_body(place, tokens, gather, slot_weight, out, held, leave):
    core, turn = place[0], place[1]
    piece = tokens.shape[2] - 256
    stores = []
    for z in range(2):
        for k in range(4):
            which = z * 4 + (core * 2 if k < 2 else 2 - core * 2) + k % 2
            part = dot(gather[...], tokens[which, :, :piece], 1, 0)
            held[z, :, k * piece : (k + 1) * piece] = part.astype(BF16)
        k = turn // 2
        which = z * 4 + jnp.where(k < 2, core * 2, 2 - core * 2) + k % 2
        dy = dot(gather[...], tokens[which, :, piece:], 1, 0) * slot_weight[...]
        held[z, :, 4 * piece :] = dy.astype(BF16)
        stores.append(pltpu.make_async_copy(held.at[z], out.at[z], leave.at[z]))
        stores[-1].start()
    for store in stores:
        store.wait()


def dispatch(place, tokens, gather, slot_weight):
    count = slot_weight.shape[0]
    vmem = pl.BlockSpec(memory_space=pltpu.VMEM)
    shape = (2, count, 4 * (tokens.shape[2] - 256) + 256)
    return pl.pallas_call(
        dispatch_body,
        in_specs=[pl.BlockSpec(memory_space=pltpu.SMEM), vmem, vmem, vmem],
        out_specs=pl.BlockSpec(memory_space=pl.ANY),
        out_shape=pltpu.HBM(shape, BF16),
        scratch_shapes=[pltpu.VMEM(shape, BF16), pltpu.SemaphoreType.DMA((2,))],
        compiler_params=params(),
        cost_estimate=cost(2 * 24 * 8 * 384 * 128, 1600000),
    )(place, tokens, gather, slot_weight)


def combine_body(place, returned, select, out):
    core = place[0]
    piece = out.shape[2]
    for z in range(2):
        for k in range(4):
            which = z * 4 + (core * 2 if k < 2 else 2 - core * 2) + k % 2
            part = returned[z, :, k * piece : (k + 1) * piece]
            out[which] = dot(select[...], part, 1, 0).astype(BF16)


def combine(place, returned, select, tensor):
    tokens = select.shape[0]
    vmem = pl.BlockSpec(memory_space=pltpu.VMEM)
    return pl.pallas_call(
        combine_body,
        in_specs=[pl.BlockSpec(memory_space=pltpu.SMEM), vmem, vmem],
        out_specs=vmem,
        out_shape=jax.ShapeDtypeStruct((tensor, tokens, 2 * returned.shape[2] // tensor), BF16),
        compiler_params=params(),
        cost_estimate=cost(2 * 24 * 128 * 3072, 1000000),
    )(place, returned, select)


def chunks(total, parts):
    step = total // parts
    return [pl.ds(i * step, step) for i in range(parts)]


def hold_body(*refs):
    count = len(refs) // 2
    for source, target in zip(refs[:count], refs[count:]):
        target[...] = source[...]


def hold(*arrays):
    vmem = pl.BlockSpec(memory_space=pltpu.VMEM)
    return pl.pallas_call(
        hold_body,
        in_specs=[vmem] * len(arrays),
        out_specs=[vmem] * len(arrays),
        out_shape=[pltpu.VMEM(array.shape, array.dtype) for array in arrays],
        compiler_params=params(),
        cost_estimate=cost(0, 2000000 * len(arrays)),
    )(*arrays)


def project_body(pairs, side, *refs):
    own, far, (act, out, fetched, partial, held, arrive, leave) = (
        refs[:pairs],
        refs[pairs : 2 * pairs],
        refs[2 * pairs :],
    )
    quarter = own[0].shape[1]
    pieces = chunks(held.shape[1], leave.shape[1])
    fetch_own = fetched.shape[0] == 2 * pairs
    sources = (list(own) if fetch_own else []) + list(far)
    loads = [
        [
            pltpu.make_async_copy(source.at[piece], fetched.at[p, piece], arrive.at[p, i])
            for i, piece in enumerate(pieces)
        ]
        for p, source in enumerate(sources)
    ]
    for group in loads:
        for load in group:
            load.start()
    near, away = pl.ds(0, quarter), pl.ds(quarter, quarter)
    near = act[:, near] if side == 1 else act[near]
    away = act[:, away] if side == 1 else act[away]
    for i, piece in enumerate(pieces):
        for p in range(pairs):
            if fetch_own:
                loads[p][i].wait()
            rows = fetched[p, piece] if fetch_own else own[p][piece]
            partial[p, piece] = dot(rows, near, 1, side)
    stores = []
    shift = pairs if fetch_own else 0
    for p in range(pairs):
        for i, piece in enumerate(pieces):
            loads[shift + p][i].wait()
            value = partial[p, piece] + dot(fetched[shift + p, piece], away, 1, side)
            held[p, piece] = value.astype(BF16)
            stores.append(
                pltpu.make_async_copy(held.at[p, piece], out.at[p, piece], leave.at[p, i])
            )
            stores[-1].start()
    for store in stores:
        store.wait()


def project(own, far, act, side, count, fetch_own):
    pairs = len(own)
    hidden, quarter = own[0].shape
    parts = 3
    vmem, hbm = pl.BlockSpec(memory_space=pltpu.VMEM), pl.BlockSpec(memory_space=pl.ANY)
    fetched = 2 * pairs if fetch_own else pairs
    return pl.pallas_call(
        functools.partial(project_body, pairs, side),
        in_specs=[hbm if fetch_own else vmem] * pairs + [hbm] * pairs + [vmem],
        out_specs=hbm,
        out_shape=pltpu.HBM((pairs, hidden, count), BF16),
        scratch_shapes=[
            pltpu.VMEM((fetched, hidden, quarter), BF16),
            pltpu.VMEM((pairs, hidden, count), F32),
            pltpu.VMEM((pairs, hidden, count), BF16),
            pltpu.SemaphoreType.DMA((fetched, parts)),
            pltpu.SemaphoreType.DMA((pairs, parts)),
        ],
        compiler_params=params(),
        cost_estimate=cost(4 * pairs * hidden * quarter * count, 4 * pairs * hidden * quarter),
    )(*(in_hbm if fetch_own else in_vmem)(*own), *in_hbm(*far), act)


def row_grad_body(
    kept, crossed, slope, active, own_gate, own_up, far_gate, far_up, out, held, leave
):
    quarter = own_gate.shape[1]
    parts = leave.shape[1]
    grad = kept[0].astype(F32) + crossed[0].astype(F32)
    gate_grad = (grad * slope[...]).T.astype(BF16)
    up_grad = (grad * active[...]).T.astype(BF16)
    stores = []
    for half, (gate, up) in enumerate(((own_gate, own_up), (far_gate, far_up))):
        for i, piece in enumerate(chunks(quarter, parts)):
            value = dot(gate_grad, gate[:, piece], 1, 0) + dot(up_grad, up[:, piece], 1, 0)
            where = pl.ds(half * quarter + i * (quarter // parts), quarter // parts)
            held[:, where] = value.astype(BF16)
            stores.append(
                pltpu.make_async_copy(held.at[:, where], out.at[:, where], leave.at[half, i])
            )
            stores[-1].start()
    for store in stores:
        store.wait()


def row_grad_product(kept, crossed, slope, active, weights):
    hidden, quarter = weights[0].shape
    count = kept.shape[2]
    parts = 3
    vmem = pl.BlockSpec(memory_space=pltpu.VMEM)
    return pl.pallas_call(
        row_grad_body,
        in_specs=[vmem] * 8,
        out_specs=pl.BlockSpec(memory_space=pl.ANY),
        out_shape=pltpu.HBM((count, 2 * quarter), BF16),
        scratch_shapes=[
            pltpu.VMEM((count, 2 * quarter), BF16),
            pltpu.SemaphoreType.DMA((2, parts)),
        ],
        compiler_params=params(),
        cost_estimate=cost(8 * hidden * quarter * count, 8 * hidden * quarter),
    )(*in_vmem(kept, crossed, slope, active, *weights))


def per_device(x_rows, cotangent, expert_ids, route_weight, gate_weight, up_weight, down_weight):
    tensor = lax.axis_size("tensor")
    experts = lax.axis_size(EXPERT)
    tokens, piece = x_rows.shape
    places = experts * CAP
    half = gate_weight.shape[1] * 2
    chunk = half // tensor
    own_gate, own_up, own_down = gate_weight[0].T, up_weight[0].T, down_weight[0]

    both = spread(x_rows, cotangent, tensor)
    both = lax.all_to_all(both, "tensor", 0, 0, tiled=True)
    select, gather, slot_weight = route_tables(expert_ids, route_weight, experts, CAP)
    place = jnp.stack([lax.axis_index("core"), lax.axis_index("tensor")]).astype(jnp.int32)
    far_gate, far_up, far_down = (
        lax.ppermute(own_gate, "core", SWAP),
        lax.ppermute(own_up, "core", SWAP),
        lax.ppermute(own_down, "core", SWAP),
    )

    sent = dispatch(place, both, gather, slot_weight).reshape(2 * experts, CAP, half + 256)
    got = lax.all_to_all(sent, SIDES, 0, 0, tiled=True).reshape(2 * places, half + 256)

    rows = 2 * places
    gate_up = project((own_gate, own_up), (far_gate, far_up), got, 1, rows, False)
    crossed = lax.ppermute(gate_up, "z_hi", SWAP)
    got_dy = lax.all_gather(got[:, half : half + chunk].T, "tensor", axis=0, tiled=True)
    hidden_grad = project((own_down,), (far_down,), got_dy, 0, rows, True)
    crossed_grad = lax.ppermute(hidden_grad, "z_hi", SWAP)
    swapped_dy = lax.ppermute(got_dy[half // 2 :], "core", SWAP)

    gate_up = gate_up.astype(F32) + crossed.astype(F32)
    gate, up = gate_up[0], gate_up[1]
    sigma = jax.nn.sigmoid(gate)
    active = gate * sigma
    hidden = (active * up).astype(BF16)
    swapped_hidden = lax.ppermute(hidden, "core", SWAP)
    slope = up * sigma * (1.0 + gate * (1.0 - sigma))

    far_gate, far_up, _ = lax.optimization_barrier((far_gate, far_up, crossed))
    far_gate, far_up = hold(*in_hbm(far_gate, far_up))
    term = row_grad_product(
        hidden_grad, crossed_grad, slope, active, (own_gate, own_up, far_gate, far_up)
    )
    returned = lax.all_to_all(
        term.reshape(2 * experts, CAP, half), SIDES, 0, 0, tiled=True
    ).reshape(2, places, half)
    mixed = combine(place, returned, select, tensor)
    mixed = lax.all_to_all(mixed, "tensor", 0, 0, tiled=True)
    input_grad = jnp.sum(mixed.astype(F32), axis=0).astype(BF16)

    down_grad = dot(hidden, got_dy[: half // 2], 1, 1) + dot(swapped_hidden, swapped_dy, 1, 1)
    return (input_grad, down_grad.astype(BF16)[None])


def solution(mesh):
    fine = Mesh(mesh.devices.reshape(2, 2, 4, 4, 8), AXES)
    placed = (
        P(BLOCKS, "tensor"),
        P(BLOCKS, "tensor"),
        P(BLOCKS, None),
        P(BLOCKS, None),
        P(EXPERT, ("z_hi", "core"), "tensor"),
        P(EXPERT, ("z_hi", "core"), "tensor"),
        P(EXPERT, "tensor", ("z_hi", "core")),
    )
    return jax.shard_map(
        per_device,
        mesh=fine,
        in_specs=placed,
        out_specs=(P(BLOCKS, "tensor"), P(EXPERT, "tensor", ("z_hi", "core"))),
        check_vma=False,
    )
```

```python
import functools

import jax
import jax.numpy as jnp
from jax import lax
from jax.experimental import pallas as pl
from jax.experimental.pallas import tpu as pltpu
from jax.sharding import Mesh, PartitionSpec as P

CAP = 8
BF16 = jnp.bfloat16
F32 = jnp.float32
AXES = ("z_hi", "core", "z_lo", "x", "tensor")
BLOCKS = ("z_hi", "core", "z_lo", "x")
EXPERT = ("z_lo", "x")
SIDES = ("z_hi", "z_lo", "x")
SWAP = [(0, 1), (1, 0)]


def route_tables(expert_ids, route_weight, experts, capacity):
    onehot = (expert_ids[:, :, None] == jnp.arange(experts, dtype=jnp.int32)[None, None, :]).astype(
        jnp.int32
    )
    per_token = jnp.sum(onehot, axis=1)
    before = jnp.cumsum(per_token, axis=0) - per_token
    slot = jnp.sum(onehot * before[:, None, :], axis=2)
    target = expert_ids * capacity + slot
    places = jnp.arange(experts * capacity, dtype=jnp.int32)
    select = jnp.sum((target[:, :, None] == places[None, None, :]).astype(F32), axis=1).astype(BF16)
    match = (target.T[None] == places[:, None, None]).astype(F32)
    gather = jnp.sum(match, axis=1).astype(BF16)
    slot_weight = jnp.sum(match * route_weight.T[None], axis=(1, 2))
    return (select, gather, slot_weight[:, None])


def dot(a, b, ca, cb):
    return lax.dot_general(a, b, (((ca,), (cb,)), ((), ())), preferred_element_type=F32)


def params():
    return pltpu.CompilerParams(vmem_limit_bytes=16 * 1024 * 1024)


def in_hbm(*arrays):
    return [pltpu.with_memory_space_constraint(array, pltpu.HBM) for array in arrays]


def in_vmem(*arrays):
    return [pltpu.with_memory_space_constraint(array, pltpu.VMEM) for array in arrays]


def cost(flops, moved):
    return pl.CostEstimate(flops=flops, bytes_accessed=moved, transcendentals=0)


def spread_body(x_rows, cotangent, out):
    tokens, piece = x_rows.shape
    half = piece // 2
    blank = jnp.zeros((tokens, out.shape[2] - piece - half), BF16)
    for j in range(2):
        part = jnp.concatenate([cotangent[:, j * half : (j + 1) * half], blank], axis=1)
        for i in range(j, out.shape[0], 2):
            out[i, :, :piece] = x_rows[...]
            out[i, :, piece:] = part


def spread(x_rows, cotangent, tensor):
    tokens, piece = x_rows.shape
    vmem = pl.BlockSpec(memory_space=pltpu.VMEM)
    return pl.pallas_call(
        spread_body,
        in_specs=[vmem] * 2,
        out_specs=vmem,
        out_shape=pltpu.HBM((tensor, tokens, piece + 256), BF16),
        compiler_params=params(),
        cost_estimate=cost(0, 600000),
    )(*in_hbm(x_rows, cotangent))


def dispatch_body(place, tokens, gather, slot_weight, out, held, leave):
    core, turn = place[0], place[1]
    piece = tokens.shape[2] - 256
    stores = []

    def leaves(z, i, where):
        stores.append(
            pltpu.make_async_copy(held.at[z, :, where], out.at[z, :, where], leave.at[z, i])
        )
        stores[-1].start()

    for z in range(2):
        for k in range(4):
            which = z * 4 + (core * 2 if k < 2 else 2 - core * 2) + k % 2
            part = dot(gather[...], tokens[which, :, :piece], 1, 0)
            held[z, :, k * piece : (k + 1) * piece] = part.astype(BF16)
            if k % 2 == 1:
                leaves(z, k // 2, pl.ds((k - 1) * piece, 2 * piece))
        k = turn // 2
        which = z * 4 + jnp.where(k < 2, core * 2, 2 - core * 2) + k % 2
        dy = dot(gather[...], tokens[which, :, piece:], 1, 0) * slot_weight[...]
        held[z, :, 4 * piece :] = dy.astype(BF16)
        leaves(z, 2, pl.ds(4 * piece, 256))
    for store in stores:
        store.wait()


def dispatch(place, tokens, gather, slot_weight):
    count = slot_weight.shape[0]
    vmem = pl.BlockSpec(memory_space=pltpu.VMEM)
    shape = (2, count, 4 * (tokens.shape[2] - 256) + 256)
    return pl.pallas_call(
        dispatch_body,
        in_specs=[pl.BlockSpec(memory_space=pltpu.SMEM), vmem, vmem, vmem],
        out_specs=pl.BlockSpec(memory_space=pl.ANY),
        out_shape=pltpu.HBM(shape, BF16),
        scratch_shapes=[pltpu.VMEM(shape, BF16), pltpu.SemaphoreType.DMA((2, 3))],
        compiler_params=params(),
        cost_estimate=cost(2 * 24 * 8 * 384 * 128, 1600000),
    )(place, tokens, gather, slot_weight)


def combine_body(place, returned, select, out, held, leave):
    core = place[0]
    piece = out.shape[2]
    stores = []
    for z in range(2):
        mixed = dot(select[...], returned[z], 1, 0).astype(BF16)
        for k in range(4):
            which = z * 4 + (core * 2 if k < 2 else 2 - core * 2) + k % 2
            held[z * 4 + k] = mixed[:, k * piece : (k + 1) * piece]
            stores.append(
                pltpu.make_async_copy(held.at[z * 4 + k], out.at[which], leave.at[z, k])
            )
            stores[-1].start()
    for store in stores:
        store.wait()


def combine(place, returned, select, tensor):
    tokens = select.shape[0]
    vmem = pl.BlockSpec(memory_space=pltpu.VMEM)
    return pl.pallas_call(
        combine_body,
        in_specs=[pl.BlockSpec(memory_space=pltpu.SMEM), vmem, vmem],
        out_specs=pl.BlockSpec(memory_space=pl.ANY),
        out_shape=pltpu.HBM((tensor, tokens, 2 * returned.shape[2] // tensor), BF16),
        scratch_shapes=[
            pltpu.VMEM((tensor, tokens, 2 * returned.shape[2] // tensor), BF16),
            pltpu.SemaphoreType.DMA((2, 4)),
        ],
        compiler_params=params(),
        cost_estimate=cost(2 * 24 * 128 * 3072, 1000000),
    )(place, returned, select)


def chunks(total, parts):
    step = total // parts
    return [pl.ds(i * step, step) for i in range(parts)]


def hold_body(*refs):
    count = len(refs) // 2
    for source, target in zip(refs[:count], refs[count:]):
        target[...] = source[...]


def hold(*arrays):
    vmem = pl.BlockSpec(memory_space=pltpu.VMEM)
    return pl.pallas_call(
        hold_body,
        in_specs=[vmem] * len(arrays),
        out_specs=[vmem] * len(arrays),
        out_shape=[pltpu.VMEM(array.shape, array.dtype) for array in arrays],
        compiler_params=params(),
        cost_estimate=cost(0, 2000000 * len(arrays)),
    )(*arrays)


def project_body(pairs, side, *refs):
    own, far, (act, out, fetched, partial, held, arrive, leave) = (
        refs[:pairs],
        refs[pairs : 2 * pairs],
        refs[2 * pairs :],
    )
    quarter = own[0].shape[1]
    pieces = chunks(held.shape[1], leave.shape[1])
    fetch_own = fetched.shape[0] == 2 * pairs
    sources = (list(own) if fetch_own else []) + list(far)
    loads = [
        [
            pltpu.make_async_copy(source.at[piece], fetched.at[p, piece], arrive.at[p, i])
            for i, piece in enumerate(pieces)
        ]
        for p, source in enumerate(sources)
    ]
    for group in loads:
        for load in group:
            load.start()
    near, away = pl.ds(0, quarter), pl.ds(quarter, quarter)
    near = act[:, near] if side == 1 else act[near]
    away = act[:, away] if side == 1 else act[away]
    for i, piece in enumerate(pieces):
        for p in range(pairs):
            if fetch_own:
                loads[p][i].wait()
            rows = fetched[p, piece] if fetch_own else own[p][piece]
            partial[p, piece] = dot(rows, near, 1, side)
    stores = []
    shift = pairs if fetch_own else 0
    for p in range(pairs):
        for i, piece in enumerate(pieces):
            loads[shift + p][i].wait()
            value = partial[p, piece] + dot(fetched[shift + p, piece], away, 1, side)
            held[p, piece] = value.astype(BF16)
            stores.append(
                pltpu.make_async_copy(held.at[p, piece], out.at[p, piece], leave.at[p, i])
            )
            stores[-1].start()
    for store in stores:
        store.wait()


def project(own, far, act, side, count, fetch_own):
    pairs = len(own)
    hidden, quarter = own[0].shape
    parts = 2
    vmem, hbm = pl.BlockSpec(memory_space=pltpu.VMEM), pl.BlockSpec(memory_space=pl.ANY)
    fetched = 2 * pairs if fetch_own else pairs
    return pl.pallas_call(
        functools.partial(project_body, pairs, side),
        in_specs=[hbm if fetch_own else vmem] * pairs + [hbm] * pairs + [vmem],
        out_specs=hbm,
        out_shape=pltpu.HBM((pairs, hidden, count), BF16),
        scratch_shapes=[
            pltpu.VMEM((fetched, hidden, quarter), BF16),
            pltpu.VMEM((pairs, hidden, count), F32),
            pltpu.VMEM((pairs, hidden, count), BF16),
            pltpu.SemaphoreType.DMA((fetched, parts)),
            pltpu.SemaphoreType.DMA((pairs, parts)),
        ],
        compiler_params=params(),
        cost_estimate=cost(4 * pairs * hidden * quarter * count, 4 * pairs * hidden * quarter),
    )(*(in_hbm if fetch_own else in_vmem)(*own), *in_hbm(*far), act)


def row_grad_body(
    kept, crossed, slope, active, own_gate, own_up, far_gate, far_up, out, held, leave
):
    quarter = own_gate.shape[1]
    parts = leave.shape[1]
    grad = kept[0].astype(F32) + crossed[0].astype(F32)
    gate_grad = (grad * slope[...]).T.astype(BF16)
    up_grad = (grad * active[...]).T.astype(BF16)
    stores = []
    for half, (gate, up) in enumerate(((own_gate, own_up), (far_gate, far_up))):
        for i, piece in enumerate(chunks(quarter, parts)):
            value = dot(gate_grad, gate[:, piece], 1, 0) + dot(up_grad, up[:, piece], 1, 0)
            where = pl.ds(half * quarter + i * (quarter // parts), quarter // parts)
            held[:, where] = value.astype(BF16)
            stores.append(
                pltpu.make_async_copy(held.at[:, where], out.at[:, where], leave.at[half, i])
            )
            stores[-1].start()
    for store in stores:
        store.wait()


def row_grad_product(kept, crossed, slope, active, weights):
    hidden, quarter = weights[0].shape
    count = kept.shape[2]
    parts = 3
    vmem = pl.BlockSpec(memory_space=pltpu.VMEM)
    return pl.pallas_call(
        row_grad_body,
        in_specs=[vmem] * 8,
        out_specs=pl.BlockSpec(memory_space=pl.ANY),
        out_shape=pltpu.HBM((count, 2 * quarter), BF16),
        scratch_shapes=[
            pltpu.VMEM((count, 2 * quarter), BF16),
            pltpu.SemaphoreType.DMA((2, parts)),
        ],
        compiler_params=params(),
        cost_estimate=cost(8 * hidden * quarter * count, 8 * hidden * quarter),
    )(*in_vmem(kept, crossed, slope, active, *weights))


def per_device(x_rows, cotangent, expert_ids, route_weight, gate_weight, up_weight, down_weight):
    tensor = lax.axis_size("tensor")
    experts = lax.axis_size(EXPERT)
    tokens, piece = x_rows.shape
    places = experts * CAP
    half = gate_weight.shape[1] * 2
    chunk = half // tensor
    own_gate, own_up, own_down = gate_weight[0].T, up_weight[0].T, down_weight[0]

    both = spread(x_rows, cotangent, tensor)
    both = lax.all_to_all(both, "tensor", 0, 0, tiled=True)
    select, gather, slot_weight = route_tables(expert_ids, route_weight, experts, CAP)
    place = jnp.stack([lax.axis_index("core"), lax.axis_index("tensor")]).astype(jnp.int32)
    far_gate, far_up, far_down = (
        lax.ppermute(own_gate, "core", SWAP),
        lax.ppermute(own_up, "core", SWAP),
        lax.ppermute(own_down, "core", SWAP),
    )

    sent = dispatch(place, both, gather, slot_weight).reshape(2 * experts, CAP, half + 256)
    got = lax.all_to_all(sent, SIDES, 0, 0, tiled=True).reshape(2 * places, half + 256)

    rows = 2 * places
    gate_up = project((own_gate, own_up), (far_gate, far_up), got, 1, rows, False)
    crossed = lax.ppermute(gate_up, "z_hi", SWAP)
    got_dy = lax.all_gather(got[:, half : half + chunk].T, "tensor", axis=0, tiled=True)
    hidden_grad = project((own_down,), (far_down,), got_dy, 0, rows, True)
    crossed_grad = lax.ppermute(hidden_grad, "z_hi", SWAP)
    swapped_dy = lax.ppermute(got_dy[half // 2 :], "core", SWAP)

    gate_up = gate_up.astype(F32) + crossed.astype(F32)
    gate, up = gate_up[0], gate_up[1]
    sigma = jax.nn.sigmoid(gate)
    active = gate * sigma
    hidden = (active * up).astype(BF16)
    swapped_hidden = lax.ppermute(hidden, "core", SWAP)
    slope = up * sigma * (1.0 + gate * (1.0 - sigma))

    far_gate, far_up, _ = lax.optimization_barrier((far_gate, far_up, crossed))
    far_gate, far_up = hold(*in_hbm(far_gate, far_up))
    term = row_grad_product(
        hidden_grad, crossed_grad, slope, active, (own_gate, own_up, far_gate, far_up)
    )
    returned = lax.all_to_all(
        term.reshape(2 * experts, CAP, half), SIDES, 0, 0, tiled=True
    ).reshape(2, places, half)
    mixed = combine(place, returned, select, tensor)
    mixed = lax.all_to_all(mixed, "tensor", 0, 0, tiled=True)
    input_grad = jnp.sum(mixed.astype(F32), axis=0).astype(BF16)

    down_grad = dot(hidden, got_dy[: half // 2], 1, 1) + dot(swapped_hidden, swapped_dy, 1, 1)
    return (input_grad, down_grad.astype(BF16)[None])


def solution(mesh):
    fine = Mesh(mesh.devices.reshape(2, 2, 4, 4, 8), AXES)
    placed = (
        P(BLOCKS, "tensor"),
        P(BLOCKS, "tensor"),
        P(BLOCKS, None),
        P(BLOCKS, None),
        P(EXPERT, ("z_hi", "core"), "tensor"),
        P(EXPERT, ("z_hi", "core"), "tensor"),
        P(EXPERT, "tensor", ("z_hi", "core")),
    )
    return jax.shard_map(
        per_device,
        mesh=fine,
        in_specs=placed,
        out_specs=(P(BLOCKS, "tensor"), P(EXPERT, "tensor", ("z_hi", "core"))),
        check_vma=False,
    )
```

```python
import functools

import jax
import jax.numpy as jnp
from jax import lax
from jax.experimental import pallas as pl
from jax.experimental.pallas import tpu as pltpu
from jax.sharding import Mesh, PartitionSpec as P

CAP = 8
BF16 = jnp.bfloat16
F32 = jnp.float32
AXES = ("z_hi", "core", "z_lo", "x", "tensor")
BLOCKS = ("z_hi", "core", "z_lo", "x")
EXPERT = ("z_lo", "x")
SIDES = ("z_hi", "z_lo", "x")
SWAP = [(0, 1), (1, 0)]


def route_tables(expert_ids, route_weight, experts, capacity):
    onehot = (expert_ids[:, :, None] == jnp.arange(experts, dtype=jnp.int32)[None, None, :]).astype(
        jnp.int32
    )
    per_token = jnp.sum(onehot, axis=1)
    before = jnp.cumsum(per_token, axis=0) - per_token
    slot = jnp.sum(onehot * before[:, None, :], axis=2)
    target = expert_ids * capacity + slot
    places = jnp.arange(experts * capacity, dtype=jnp.int32)
    select = jnp.sum((target[:, :, None] == places[None, None, :]).astype(F32), axis=1).astype(BF16)
    match = (target.T[None] == places[:, None, None]).astype(F32)
    gather = jnp.sum(match, axis=1).astype(BF16)
    slot_weight = jnp.sum(match * route_weight.T[None], axis=(1, 2))
    return (select, gather, slot_weight[:, None])


def dot(a, b, ca, cb):
    return lax.dot_general(a, b, (((ca,), (cb,)), ((), ())), preferred_element_type=F32)


def params():
    return pltpu.CompilerParams(vmem_limit_bytes=16 * 1024 * 1024)


def in_hbm(*arrays):
    return [pltpu.with_memory_space_constraint(array, pltpu.HBM) for array in arrays]


def in_vmem(*arrays):
    return [pltpu.with_memory_space_constraint(array, pltpu.VMEM) for array in arrays]


def cost(flops, moved):
    return pl.CostEstimate(flops=flops, bytes_accessed=moved, transcendentals=0)


def spread_body(x_rows, cotangent, out):
    tokens, piece = x_rows.shape
    half = piece // 2
    blank = jnp.zeros((tokens, out.shape[2] - piece - half), BF16)
    for j in range(2):
        part = jnp.concatenate([cotangent[:, j * half : (j + 1) * half], blank], axis=1)
        for i in range(j, out.shape[0], 2):
            out[i, :, :piece] = x_rows[...]
            out[i, :, piece:] = part


def spread(x_rows, cotangent, tensor):
    tokens, piece = x_rows.shape
    vmem = pl.BlockSpec(memory_space=pltpu.VMEM)
    return pl.pallas_call(
        spread_body,
        in_specs=[vmem] * 2,
        out_specs=vmem,
        out_shape=pltpu.HBM((tensor, tokens, piece + 256), BF16),
        compiler_params=params(),
        cost_estimate=cost(0, 600000),
    )(*in_hbm(x_rows, cotangent))


def dispatch_body(place, tokens, gather, slot_weight, out, held, leave):
    core, turn = place[0], place[1]
    piece = tokens.shape[2] - 256
    stores = []

    def leaves(z, i, where):
        stores.append(
            pltpu.make_async_copy(held.at[z, :, where], out.at[z, :, where], leave.at[z, i])
        )
        stores[-1].start()

    for z in range(2):
        for k in range(4):
            which = z * 4 + (core * 2 if k < 2 else 2 - core * 2) + k % 2
            part = dot(gather[...], tokens[which, :, :piece], 1, 0)
            held[z, :, k * piece : (k + 1) * piece] = part.astype(BF16)
            if k % 2 == 1:
                leaves(z, k // 2, pl.ds((k - 1) * piece, 2 * piece))
        k = turn // 2
        which = z * 4 + jnp.where(k < 2, core * 2, 2 - core * 2) + k % 2
        dy = dot(gather[...], tokens[which, :, piece:], 1, 0) * slot_weight[...]
        held[z, :, 4 * piece :] = dy.astype(BF16)
        leaves(z, 2, pl.ds(4 * piece, 256))
    for store in stores:
        store.wait()


def dispatch(place, tokens, gather, slot_weight):
    count = slot_weight.shape[0]
    vmem = pl.BlockSpec(memory_space=pltpu.VMEM)
    shape = (2, count, 4 * (tokens.shape[2] - 256) + 256)
    return pl.pallas_call(
        dispatch_body,
        in_specs=[pl.BlockSpec(memory_space=pltpu.SMEM), vmem, vmem, vmem],
        out_specs=pl.BlockSpec(memory_space=pl.ANY),
        out_shape=pltpu.HBM(shape, BF16),
        scratch_shapes=[pltpu.VMEM(shape, BF16), pltpu.SemaphoreType.DMA((2, 3))],
        compiler_params=params(),
        cost_estimate=cost(2 * 24 * 8 * 384 * 128, 1600000),
    )(place, tokens, gather, slot_weight)


def combine_body(place, returned, select, out, held, leave):
    core = place[0]
    piece = out.shape[2]
    stores = []
    for z in range(2):
        mixed = dot(select[...], returned[z], 1, 0).astype(BF16)
        for k in range(4):
            which = z * 4 + (core * 2 if k < 2 else 2 - core * 2) + k % 2
            held[z * 4 + k] = mixed[:, k * piece : (k + 1) * piece]
            stores.append(
                pltpu.make_async_copy(held.at[z * 4 + k], out.at[which], leave.at[z, k])
            )
            stores[-1].start()
    for store in stores:
        store.wait()


def combine(place, returned, select, tensor):
    tokens = select.shape[0]
    vmem = pl.BlockSpec(memory_space=pltpu.VMEM)
    return pl.pallas_call(
        combine_body,
        in_specs=[pl.BlockSpec(memory_space=pltpu.SMEM), vmem, vmem],
        out_specs=pl.BlockSpec(memory_space=pl.ANY),
        out_shape=pltpu.HBM((tensor, tokens, 2 * returned.shape[2] // tensor), BF16),
        scratch_shapes=[
            pltpu.VMEM((tensor, tokens, 2 * returned.shape[2] // tensor), BF16),
            pltpu.SemaphoreType.DMA((2, 4)),
        ],
        compiler_params=params(),
        cost_estimate=cost(2 * 24 * 128 * 3072, 1000000),
    )(place, returned, select)


def chunks(total, parts):
    step = total // parts
    return [pl.ds(i * step, step) for i in range(parts)]


def hold_body(*refs):
    count = len(refs) // 2
    for source, target in zip(refs[:count], refs[count:]):
        target[...] = source[...]


def hold(*arrays):
    vmem = pl.BlockSpec(memory_space=pltpu.VMEM)
    return pl.pallas_call(
        hold_body,
        in_specs=[vmem] * len(arrays),
        out_specs=[vmem] * len(arrays),
        out_shape=[pltpu.VMEM(array.shape, array.dtype) for array in arrays],
        compiler_params=params(),
        cost_estimate=cost(0, 2000000 * len(arrays)),
    )(*arrays)


def project_body(pairs, side, *refs):
    own, far, (act, out, fetched, partial, held, arrive, leave) = (
        refs[:pairs],
        refs[pairs : 2 * pairs],
        refs[2 * pairs :],
    )
    quarter = own[0].shape[1]
    pieces = chunks(held.shape[1], leave.shape[1])
    fetch_own = fetched.shape[0] == 2 * pairs
    sources = (list(own) if fetch_own else []) + list(far)
    loads = [
        [
            pltpu.make_async_copy(source.at[piece], fetched.at[p, piece], arrive.at[p, i])
            for i, piece in enumerate(pieces)
        ]
        for p, source in enumerate(sources)
    ]
    for group in loads:
        for load in group:
            load.start()
    near, away = pl.ds(0, quarter), pl.ds(quarter, quarter)
    near = act[:, near] if side == 1 else act[near]
    away = act[:, away] if side == 1 else act[away]
    for i, piece in enumerate(pieces):
        for p in range(pairs):
            if fetch_own:
                loads[p][i].wait()
            rows = fetched[p, piece] if fetch_own else own[p][piece]
            partial[p, piece] = dot(rows, near, 1, side)
    stores = []
    shift = pairs if fetch_own else 0
    for p in range(pairs):
        for i, piece in enumerate(pieces):
            loads[shift + p][i].wait()
            value = partial[p, piece] + dot(fetched[shift + p, piece], away, 1, side)
            held[p, piece] = value.astype(BF16)
            stores.append(
                pltpu.make_async_copy(held.at[p, piece], out.at[p, piece], leave.at[p, i])
            )
            stores[-1].start()
    for store in stores:
        store.wait()


def project(own, far, act, side, count, fetch_own):
    pairs = len(own)
    hidden, quarter = own[0].shape
    parts = 2
    vmem, hbm = pl.BlockSpec(memory_space=pltpu.VMEM), pl.BlockSpec(memory_space=pl.ANY)
    fetched = 2 * pairs if fetch_own else pairs
    return pl.pallas_call(
        functools.partial(project_body, pairs, side),
        in_specs=[hbm if fetch_own else vmem] * pairs + [hbm] * pairs + [vmem],
        out_specs=hbm,
        out_shape=pltpu.HBM((pairs, hidden, count), BF16),
        scratch_shapes=[
            pltpu.VMEM((fetched, hidden, quarter), BF16),
            pltpu.VMEM((pairs, hidden, count), F32),
            pltpu.VMEM((pairs, hidden, count), BF16),
            pltpu.SemaphoreType.DMA((fetched, parts)),
            pltpu.SemaphoreType.DMA((pairs, parts)),
        ],
        compiler_params=params(),
        cost_estimate=cost(4 * pairs * hidden * quarter * count, 4 * pairs * hidden * quarter),
    )(*(in_hbm if fetch_own else in_vmem)(*own), *in_hbm(*far), act)


def row_grad_body(
    kept, crossed, slope, active, own_gate, own_up, far_gate, far_up, out, held, leave
):
    quarter = own_gate.shape[1]
    parts = leave.shape[1]
    grad = kept[0].astype(F32) + crossed[0].astype(F32)
    gate_grad = (grad * slope[...]).astype(BF16).T
    up_grad = (grad * active[...]).astype(BF16).T
    stores = []
    for half, (gate, up) in enumerate(((own_gate, own_up), (far_gate, far_up))):
        for i, piece in enumerate(chunks(quarter, parts)):
            value = dot(gate_grad, gate[:, piece], 1, 0) + dot(up_grad, up[:, piece], 1, 0)
            where = pl.ds(half * quarter + i * (quarter // parts), quarter // parts)
            held[:, where] = value.astype(BF16)
            stores.append(
                pltpu.make_async_copy(held.at[:, where], out.at[:, where], leave.at[half, i])
            )
            stores[-1].start()
    for store in stores:
        store.wait()


def row_grad_product(kept, crossed, slope, active, weights):
    hidden, quarter = weights[0].shape
    count = kept.shape[2]
    parts = 3
    vmem = pl.BlockSpec(memory_space=pltpu.VMEM)
    return pl.pallas_call(
        row_grad_body,
        in_specs=[vmem] * 8,
        out_specs=pl.BlockSpec(memory_space=pl.ANY),
        out_shape=pltpu.HBM((count, 2 * quarter), BF16),
        scratch_shapes=[
            pltpu.VMEM((count, 2 * quarter), BF16),
            pltpu.SemaphoreType.DMA((2, parts)),
        ],
        compiler_params=params(),
        cost_estimate=cost(8 * hidden * quarter * count, 8 * hidden * quarter),
    )(*in_vmem(kept, crossed, slope, active, *weights))


def per_device(x_rows, cotangent, expert_ids, route_weight, gate_weight, up_weight, down_weight):
    tensor = lax.axis_size("tensor")
    experts = lax.axis_size(EXPERT)
    tokens, piece = x_rows.shape
    places = experts * CAP
    half = gate_weight.shape[1] * 2
    chunk = half // tensor
    hidden_units = gate_weight.shape[2]
    own_gate, own_up, own_down = gate_weight[0].T, up_weight[0].T, down_weight[0]

    both = spread(x_rows, cotangent, tensor)
    both = lax.all_to_all(both, "tensor", 0, 0, tiled=True)
    select, gather, slot_weight = route_tables(expert_ids, route_weight, experts, CAP)
    place = jnp.stack([lax.axis_index("core"), lax.axis_index("tensor")]).astype(jnp.int32)
    far_gate, far_up, far_down = (
        lax.ppermute(own_gate, "core", SWAP),
        lax.ppermute(own_up, "core", SWAP),
        lax.ppermute(own_down, "core", SWAP),
    )

    sent = dispatch(place, both, gather, slot_weight).reshape(2 * experts, CAP, half + 256)
    got = lax.all_to_all(sent, SIDES, 0, 0, tiled=True).reshape(2 * places, half + 256)

    rows = 2 * places
    gate_up = project((own_gate, own_up), (far_gate, far_up), got, 1, rows, False)
    crossed = lax.ppermute(gate_up, "z_hi", SWAP)
    got_dy = lax.all_gather(got[:, half : half + chunk].T, "tensor", axis=0, tiled=True)
    hidden_grad = project((own_down,), (far_down,), got_dy, 0, rows, True)
    crossed_grad = lax.ppermute(hidden_grad, "z_hi", SWAP)

    gate_up = gate_up.astype(F32) + crossed.astype(F32)
    gate, up = gate_up[0], gate_up[1]
    sigma = jax.nn.sigmoid(gate)
    active = gate * sigma
    hidden = (active * up).astype(BF16)
    swapped = lax.ppermute(
        jnp.concatenate([hidden, got_dy[half // 2 :]], axis=0), "core", SWAP
    )
    swapped_hidden, swapped_dy = swapped[:hidden_units], swapped[hidden_units:]
    slope = up * sigma * (1.0 + gate * (1.0 - sigma))

    far_gate, far_up, _ = lax.optimization_barrier((far_gate, far_up, crossed))
    far_gate, far_up = hold(*in_hbm(far_gate, far_up))
    term = row_grad_product(
        hidden_grad, crossed_grad, slope, active, (own_gate, own_up, far_gate, far_up)
    )
    returned = lax.all_to_all(
        term.reshape(2 * experts, CAP, half), SIDES, 0, 0, tiled=True
    ).reshape(2, places, half)
    mixed = combine(place, returned, select, tensor)
    mixed = lax.all_to_all(mixed, "tensor", 0, 0, tiled=True)
    input_grad = jnp.sum(mixed.astype(F32), axis=0).astype(BF16)

    down_grad = dot(hidden, got_dy[: half // 2], 1, 1) + dot(swapped_hidden, swapped_dy, 1, 1)
    return (input_grad, down_grad.astype(BF16)[None])


def solution(mesh):
    fine = Mesh(mesh.devices.reshape(2, 2, 4, 4, 8), AXES)
    placed = (
        P(BLOCKS, "tensor"),
        P(BLOCKS, "tensor"),
        P(BLOCKS, None),
        P(BLOCKS, None),
        P(EXPERT, ("z_hi", "core"), "tensor"),
        P(EXPERT, ("z_hi", "core"), "tensor"),
        P(EXPERT, "tensor", ("z_hi", "core")),
    )
    return jax.shard_map(
        per_device,
        mesh=fine,
        in_specs=placed,
        out_specs=(P(BLOCKS, "tensor"), P(EXPERT, "tensor", ("z_hi", "core"))),
        check_vma=False,
    )
```

```python
import functools

import jax
import jax.numpy as jnp
from jax import lax
from jax.experimental import pallas as pl
from jax.experimental.pallas import tpu as pltpu
from jax.sharding import Mesh, PartitionSpec as P

CAP = 8
BF16 = jnp.bfloat16
F32 = jnp.float32
AXES = ("z_hi", "core", "z_lo", "x", "tensor")
BLOCKS = ("z_hi", "core", "z_lo", "x")
EXPERT = ("z_lo", "x")
SIDES = ("z_hi", "z_lo", "x")
SWAP = [(0, 1), (1, 0)]


def route_tables(expert_ids, route_weight, experts, capacity):
    onehot = (expert_ids[:, :, None] == jnp.arange(experts, dtype=jnp.int32)[None, None, :]).astype(
        jnp.int32
    )
    per_token = jnp.sum(onehot, axis=1)
    before = jnp.cumsum(per_token, axis=0) - per_token
    slot = jnp.sum(onehot * before[:, None, :], axis=2)
    target = expert_ids * capacity + slot
    places = jnp.arange(experts * capacity, dtype=jnp.int32)
    select = jnp.sum((target[:, :, None] == places[None, None, :]).astype(F32), axis=1).astype(BF16)
    match = (target.T[None] == places[:, None, None]).astype(F32)
    gather = jnp.sum(match, axis=1).astype(BF16)
    slot_weight = jnp.sum(match * route_weight.T[None], axis=(1, 2))
    return (select, gather, slot_weight[:, None])


def dot(a, b, ca, cb):
    return lax.dot_general(a, b, (((ca,), (cb,)), ((), ())), preferred_element_type=F32)


def params():
    return pltpu.CompilerParams(vmem_limit_bytes=16 * 1024 * 1024)


def in_hbm(*arrays):
    return [pltpu.with_memory_space_constraint(array, pltpu.HBM) for array in arrays]


def in_vmem(*arrays):
    return [pltpu.with_memory_space_constraint(array, pltpu.VMEM) for array in arrays]


def cost(flops, moved):
    return pl.CostEstimate(flops=flops, bytes_accessed=moved, transcendentals=0)


def spread_body(x_rows, cotangent, out):
    tokens, piece = x_rows.shape
    half = piece // 2
    blank = jnp.zeros((tokens, out.shape[2] - piece - half), BF16)
    for j in range(2):
        part = jnp.concatenate([cotangent[:, j * half : (j + 1) * half], blank], axis=1)
        for i in range(j, out.shape[0], 2):
            out[i, :, :piece] = x_rows[...]
            out[i, :, piece:] = part


def spread(x_rows, cotangent, tensor):
    tokens, piece = x_rows.shape
    vmem = pl.BlockSpec(memory_space=pltpu.VMEM)
    return pl.pallas_call(
        spread_body,
        in_specs=[vmem] * 2,
        out_specs=vmem,
        out_shape=pltpu.HBM((tensor, tokens, piece + 256), BF16),
        compiler_params=params(),
        cost_estimate=cost(0, 600000),
    )(*in_hbm(x_rows, cotangent))


def dispatch_body(place, tokens, gather, slot_weight, out, held, leave):
    core, turn = place[0], place[1]
    piece = tokens.shape[2] - 256
    stores = []

    def leaves(z, i, where):
        stores.append(
            pltpu.make_async_copy(held.at[z, :, where], out.at[z, :, where], leave.at[z, i])
        )
        stores[-1].start()

    for z in range(2):
        for k in range(4):
            which = z * 4 + (core * 2 if k < 2 else 2 - core * 2) + k % 2
            part = dot(gather[...], tokens[which, :, :piece], 1, 0)
            held[z, :, k * piece : (k + 1) * piece] = part.astype(BF16)
            if k % 2 == 1:
                leaves(z, k // 2, pl.ds((k - 1) * piece, 2 * piece))
        k = turn // 2
        which = z * 4 + jnp.where(k < 2, core * 2, 2 - core * 2) + k % 2
        dy = dot(gather[...], tokens[which, :, piece:], 1, 0) * slot_weight[...]
        held[z, :, 4 * piece :] = dy.astype(BF16)
        leaves(z, 2, pl.ds(4 * piece, 256))
    for store in stores:
        store.wait()


def dispatch(place, tokens, gather, slot_weight):
    count = slot_weight.shape[0]
    vmem = pl.BlockSpec(memory_space=pltpu.VMEM)
    shape = (2, count, 4 * (tokens.shape[2] - 256) + 256)
    return pl.pallas_call(
        dispatch_body,
        in_specs=[pl.BlockSpec(memory_space=pltpu.SMEM), vmem, vmem, vmem],
        out_specs=pl.BlockSpec(memory_space=pl.ANY),
        out_shape=pltpu.HBM(shape, BF16),
        scratch_shapes=[pltpu.VMEM(shape, BF16), pltpu.SemaphoreType.DMA((2, 3))],
        compiler_params=params(),
        cost_estimate=cost(2 * 24 * 8 * 384 * 128, 1600000),
    )(place, tokens, gather, slot_weight)


def combine_body(place, returned, select, out, held, leave):
    core = place[0]
    piece = out.shape[2]
    stores = []
    for z in range(2):
        mixed = dot(select[...], returned[z], 1, 0).astype(BF16)
        for k in range(4):
            which = z * 4 + (core * 2 if k < 2 else 2 - core * 2) + k % 2
            held[z * 4 + k] = mixed[:, k * piece : (k + 1) * piece]
            stores.append(
                pltpu.make_async_copy(held.at[z * 4 + k], out.at[which], leave.at[z, k])
            )
            stores[-1].start()
    for store in stores:
        store.wait()


def combine(place, returned, select, tensor):
    tokens = select.shape[0]
    vmem = pl.BlockSpec(memory_space=pltpu.VMEM)
    return pl.pallas_call(
        combine_body,
        in_specs=[pl.BlockSpec(memory_space=pltpu.SMEM), vmem, vmem],
        out_specs=pl.BlockSpec(memory_space=pl.ANY),
        out_shape=pltpu.HBM((tensor, tokens, 2 * returned.shape[2] // tensor), BF16),
        scratch_shapes=[
            pltpu.VMEM((tensor, tokens, 2 * returned.shape[2] // tensor), BF16),
            pltpu.SemaphoreType.DMA((2, 4)),
        ],
        compiler_params=params(),
        cost_estimate=cost(2 * 24 * 128 * 3072, 1000000),
    )(place, returned, select)


def chunks(total, parts):
    step = total // parts
    return [pl.ds(i * step, step) for i in range(parts)]


def hold_body(*refs):
    count = len(refs) // 2
    for source, target in zip(refs[:count], refs[count:]):
        target[...] = source[...]


def hold(*arrays):
    vmem = pl.BlockSpec(memory_space=pltpu.VMEM)
    return pl.pallas_call(
        hold_body,
        in_specs=[vmem] * len(arrays),
        out_specs=[vmem] * len(arrays),
        out_shape=[pltpu.VMEM(array.shape, array.dtype) for array in arrays],
        compiler_params=params(),
        cost_estimate=cost(0, 2000000 * len(arrays)),
    )(*arrays)


def project_body(pairs, side, *refs):
    own, far, (act, out, turned, fetched, partial, held, arrive, leave) = (
        refs[:pairs],
        refs[pairs : 2 * pairs],
        refs[2 * pairs :],
    )
    quarter = own[0].shape[1]
    pieces = chunks(held.shape[1], leave.shape[1])
    fetch_own = fetched.shape[0] == 2 * pairs
    sources = (list(own) if fetch_own else []) + list(far)
    loads = [
        [
            pltpu.make_async_copy(source.at[piece], fetched.at[p, piece], arrive.at[p, i])
            for i, piece in enumerate(pieces)
        ]
        for p, source in enumerate(sources)
    ]
    for group in loads:
        for load in group:
            load.start()
    near, away = pl.ds(0, quarter), pl.ds(quarter, quarter)
    near = act[:, near] if side == 1 else act[near]
    away = act[:, away] if side == 1 else act[away]
    for i, piece in enumerate(pieces):
        for p in range(pairs):
            if fetch_own:
                loads[p][i].wait()
            rows = fetched[p, piece] if fetch_own else own[p][piece]
            partial[p, piece] = dot(rows, near, 1, side)
    if side == 1:
        turned[...] = act[:, 2 * quarter :].T[: turned.shape[0]]
    else:
        turned[...] = jnp.zeros_like(turned)
    stores = []
    shift = pairs if fetch_own else 0
    for p in range(pairs):
        for i, piece in enumerate(pieces):
            loads[shift + p][i].wait()
            value = partial[p, piece] + dot(fetched[shift + p, piece], away, 1, side)
            held[p, piece] = value.astype(BF16)
            stores.append(
                pltpu.make_async_copy(held.at[p, piece], out.at[p, piece], leave.at[p, i])
            )
            stores[-1].start()
    for store in stores:
        store.wait()


def project(own, far, act, side, count, fetch_own, tail=16):
    pairs = len(own)
    hidden, quarter = own[0].shape
    parts = 2
    vmem, hbm = pl.BlockSpec(memory_space=pltpu.VMEM), pl.BlockSpec(memory_space=pl.ANY)
    fetched = 2 * pairs if fetch_own else pairs
    return pl.pallas_call(
        functools.partial(project_body, pairs, side),
        in_specs=[hbm if fetch_own else vmem] * pairs + [hbm] * pairs + [vmem],
        out_specs=[hbm, vmem],
        out_shape=[
            pltpu.HBM((pairs, hidden, count), BF16),
            jax.ShapeDtypeStruct((tail, count), BF16),
        ],
        scratch_shapes=[
            pltpu.VMEM((fetched, hidden, quarter), BF16),
            pltpu.VMEM((pairs, hidden, count), F32),
            pltpu.VMEM((pairs, hidden, count), BF16),
            pltpu.SemaphoreType.DMA((fetched, parts)),
            pltpu.SemaphoreType.DMA((pairs, parts)),
        ],
        compiler_params=params(),
        cost_estimate=cost(4 * pairs * hidden * quarter * count, 4 * pairs * hidden * quarter),
    )(*(in_hbm if fetch_own else in_vmem)(*own), *in_hbm(*far), act)


def row_grad_body(
    kept, crossed, slope, active, own_gate, own_up, far_gate, far_up, out, held, leave
):
    quarter = own_gate.shape[1]
    parts = leave.shape[1]
    grad = kept[0].astype(F32) + crossed[0].astype(F32)
    gate_grad = (grad * slope[...]).astype(BF16).T
    up_grad = (grad * active[...]).astype(BF16).T
    stores = []
    for half, (gate, up) in enumerate(((own_gate, own_up), (far_gate, far_up))):
        for i, piece in enumerate(chunks(quarter, parts)):
            value = dot(gate_grad, gate[:, piece], 1, 0) + dot(up_grad, up[:, piece], 1, 0)
            where = pl.ds(half * quarter + i * (quarter // parts), quarter // parts)
            held[:, where] = value.astype(BF16)
            stores.append(
                pltpu.make_async_copy(held.at[:, where], out.at[:, where], leave.at[half, i])
            )
            stores[-1].start()
    for store in stores:
        store.wait()


def row_grad_product(kept, crossed, slope, active, weights):
    hidden, quarter = weights[0].shape
    count = kept.shape[2]
    parts = 3
    vmem = pl.BlockSpec(memory_space=pltpu.VMEM)
    return pl.pallas_call(
        row_grad_body,
        in_specs=[vmem] * 8,
        out_specs=pl.BlockSpec(memory_space=pl.ANY),
        out_shape=pltpu.HBM((count, 2 * quarter), BF16),
        scratch_shapes=[
            pltpu.VMEM((count, 2 * quarter), BF16),
            pltpu.SemaphoreType.DMA((2, parts)),
        ],
        compiler_params=params(),
        cost_estimate=cost(8 * hidden * quarter * count, 8 * hidden * quarter),
    )(*in_vmem(kept, crossed, slope, active, *weights))


def per_device(x_rows, cotangent, expert_ids, route_weight, gate_weight, up_weight, down_weight):
    tensor = lax.axis_size("tensor")
    experts = lax.axis_size(EXPERT)
    tokens, piece = x_rows.shape
    places = experts * CAP
    half = gate_weight.shape[1] * 2
    chunk = half // tensor
    hidden_units = gate_weight.shape[2]
    own_gate, own_up, own_down = gate_weight[0].T, up_weight[0].T, down_weight[0]

    both = spread(x_rows, cotangent, tensor)
    both = lax.all_to_all(both, "tensor", 0, 0, tiled=True)
    select, gather, slot_weight = route_tables(expert_ids, route_weight, experts, CAP)
    place = jnp.stack([lax.axis_index("core"), lax.axis_index("tensor")]).astype(jnp.int32)
    far_gate, far_up, far_down = (
        lax.ppermute(own_gate, "core", SWAP),
        lax.ppermute(own_up, "core", SWAP),
        lax.ppermute(own_down, "core", SWAP),
    )

    sent = dispatch(place, both, gather, slot_weight).reshape(2 * experts, CAP, half + 256)
    got = lax.all_to_all(sent, SIDES, 0, 0, tiled=True).reshape(2 * places, half + 256)

    rows = 2 * places
    gate_up, dy_chunk = project((own_gate, own_up), (far_gate, far_up), got, 1, rows, False, chunk)
    crossed = lax.ppermute(gate_up, "z_hi", SWAP)
    got_dy = lax.all_gather(dy_chunk, "tensor", axis=0, tiled=True)
    hidden_grad, _ = project((own_down,), (far_down,), got_dy, 0, rows, True)
    crossed_grad = lax.ppermute(hidden_grad, "z_hi", SWAP)

    gate_up = gate_up.astype(F32) + crossed.astype(F32)
    gate, up = gate_up[0], gate_up[1]
    sigma = jax.nn.sigmoid(gate)
    active = gate * sigma
    hidden = (active * up).astype(BF16)
    swapped = lax.ppermute(
        jnp.concatenate([hidden, got_dy[half // 2 :]], axis=0), "core", SWAP
    )
    swapped_hidden, swapped_dy = swapped[:hidden_units], swapped[hidden_units:]
    slope = up * sigma * (1.0 + gate * (1.0 - sigma))

    far_gate, far_up, _ = lax.optimization_barrier((far_gate, far_up, crossed))
    far_gate, far_up = hold(*in_hbm(far_gate, far_up))
    term = row_grad_product(
        hidden_grad, crossed_grad, slope, active, (own_gate, own_up, far_gate, far_up)
    )
    returned = lax.all_to_all(
        term.reshape(2 * experts, CAP, half), SIDES, 0, 0, tiled=True
    ).reshape(2, places, half)
    mixed = combine(place, returned, select, tensor)
    mixed = lax.all_to_all(mixed, "tensor", 0, 0, tiled=True)
    input_grad = jnp.sum(mixed.astype(F32), axis=0).astype(BF16)

    down_grad = dot(hidden, got_dy[: half // 2], 1, 1) + dot(swapped_hidden, swapped_dy, 1, 1)
    return (input_grad, down_grad.astype(BF16)[None])


def solution(mesh):
    fine = Mesh(mesh.devices.reshape(2, 2, 4, 4, 8), AXES)
    placed = (
        P(BLOCKS, "tensor"),
        P(BLOCKS, "tensor"),
        P(BLOCKS, None),
        P(BLOCKS, None),
        P(EXPERT, ("z_hi", "core"), "tensor"),
        P(EXPERT, ("z_hi", "core"), "tensor"),
        P(EXPERT, "tensor", ("z_hi", "core")),
    )
    return jax.shard_map(
        per_device,
        mesh=fine,
        in_specs=placed,
        out_specs=(P(BLOCKS, "tensor"), P(EXPERT, "tensor", ("z_hi", "core"))),
        check_vma=False,
    )
```
